32 devices in a mesh: tm: 4 (over y, x), pairs: 8 (over z, core).
Axes of the slice: x: 2, y: 2, z: 4, core: 2. Of those that a mesh axis runs over, the one named last changes fastest.
Arguments:
- panels: bfloat16 [48, 4, 512, 128], P('tm', None, 'pairs')
- pair_list: int32 [2, 32768], P(None, ('tm', 'pairs')), may hold values from 0 to 2047, as said below
- pair_count: int32 [32], P(('tm', 'pairs')), may hold values from 1 to 1024, as said below
Outputs:
- stacks: float32 [32768, 512], P(('tm', 'pairs'))
The draws below stay inside these ranges and needn't reach their ends.
Inputs may be any that keep to these rules, and one draw needn't show every extreme that they name: `pair_list`: slots o * 1024 to (o + 1) * 1024 - 1 belong to owner o. The first channel of each is one of channels o * 64 to (o + 1) * 64 - 1; the second lies 1 to 100 channels after it, in the same section of 512 channels. A distance of 100 occurs in every draw. Owner o's live slots are its first pair_count[o]. Some owner has all 1024 live in every draw.
All inputs are finite; a program needn't handle non-finite values.
Results may differ from the reference program's by a relative error of at most 0.015.
Values may be sent and summed in bfloat16 or wider, within the bound.
A program may use at most 128 MiB of HBM per device.

```python
import math
import jax
import jax.numpy as jnp
from jax import lax

CH_DEV = 64
NB = 100
SEG = 512
SEGS = 12
TILE = 128
PAIR_CAP = 1024
SECTIONS = 4
SECTION = 512
OWNERS = 32
CHANNELS = 2048
NTILE = 48


def draw_panels(key, part):
    subkeys = jax.random.split(key, 3)
    full_shape = (NTILE, SECTIONS, SECTION, TILE)
    noise_part = jax.random.normal(subkeys[0], full_shape, jnp.float32)
    channel_scale = jnp.exp(jax.random.uniform(subkeys[1], (1, SECTIONS, SECTION, 1), jnp.float32, 0.0, jnp.log(10.0)))
    tile_scale = jnp.exp(jax.random.uniform(subkeys[2], (NTILE, SECTIONS, SECTION, 1), jnp.float32, 0.0, jnp.log(10.0)))
    return (noise_part * channel_scale * tile_scale).astype(jnp.bfloat16)


def draw_pair_list(key, part):
    subkeys = jax.random.split(key, 2)
    slot_ids = jnp.arange(OWNERS * PAIR_CAP, dtype=jnp.int32)
    owner_ids = slot_ids // PAIR_CAP
    within = owner_ids % (SECTION // CH_DEV)
    last_block = (within == SECTION // CH_DEV - 1).astype(jnp.int32)
    local_first = jax.random.randint(subkeys[0], slot_ids.shape, 0, CH_DEV - last_block)
    position = within * CH_DEV + local_first
    reach_max = jnp.minimum(SECTION - 1 - position, NB)
    raw_step = jax.random.randint(subkeys[1], slot_ids.shape, 0, 1 << 20)
    distance = 1 + raw_step % reach_max
    distance = jnp.where(slot_ids % PAIR_CAP == 0, reach_max, distance)
    firsts = owner_ids * CH_DEV + local_first
    return jnp.stack([firsts, firsts + distance]).astype(jnp.int32)


def draw_pair_count(key, part):
    subkeys = jax.random.split(key, 3)
    base_count = jax.random.randint(subkeys[0], (OWNERS,), PAIR_CAP // 4, PAIR_CAP + 1)
    divisor = 1 + jax.random.randint(subkeys[1], (OWNERS,), 0, 3)
    counts = base_count // divisor
    busiest = jax.random.randint(subkeys[2], (), 0, OWNERS)
    counts = jnp.where(jnp.arange(OWNERS, dtype=jnp.int32) == busiest, PAIR_CAP, counts)
    return counts.astype(jnp.int32)


def setup_inputs(seed: int = 0) -> dict:
    key_of = jax.random.split(jax.random.key(seed), 4)
    panels = draw_panels(jax.random.fold_in(key_of[3], 71), 0)
    pair_list = draw_pair_list(jax.random.fold_in(key_of[3], 71), 0)
    pair_count = draw_pair_count(jax.random.fold_in(key_of[3], 71), 0)
    return {"panels": panels, "pair_list": pair_list, "pair_count": pair_count}


def reference(panels, pair_list, pair_count):
    samples = jnp.transpose(panels, (1, 2, 0, 3)).reshape(CHANNELS, SEGS, SEG).astype(jnp.float32)
    mean_square = lax.optimization_barrier(jnp.mean(samples * samples, axis=2, keepdims=True))
    scaled = lax.optimization_barrier((samples * lax.rsqrt(mean_square + 1e-05)).astype(jnp.bfloat16))
    spectrum = jnp.fft.rfft(scaled.astype(jnp.float32), n=2 * SEG, axis=2)[:, :, :SEG] / math.sqrt(SEG)
    real_part = jnp.real(spectrum)
    imag_part = jnp.imag(spectrum)
    level_power = lax.optimization_barrier(jnp.mean(real_part * real_part + imag_part * imag_part, axis=1, keepdims=True))
    weight_gain = 1.0 / jnp.sqrt(level_power + 0.5)
    whitened = jnp.concatenate([real_part * weight_gain, imag_part * weight_gain], axis=2).astype(jnp.bfloat16)
    firsts = pair_list[0].reshape(OWNERS, PAIR_CAP)
    seconds = pair_list[1].reshape(OWNERS, PAIR_CAP)

    def one_owner(pair_block):
        first_ids, second_ids, live_count = pair_block
        left_rows = jnp.take(whitened, first_ids, axis=0).astype(jnp.float32)
        right_rows = jnp.take(whitened, second_ids, axis=0).astype(jnp.float32)
        left_real = left_rows[:, :, :SEG]
        left_imag = left_rows[:, :, SEG:]
        right_real = right_rows[:, :, :SEG]
        right_imag = right_rows[:, :, SEG:]
        cross_real = lax.optimization_barrier(jnp.mean(left_real * right_real + left_imag * right_imag, axis=1))
        cross_imag = lax.optimization_barrier(jnp.mean(left_imag * right_real - left_real * right_imag, axis=1))
        cross_spec = lax.optimization_barrier(jnp.concatenate([cross_real, cross_imag], axis=1).astype(jnp.bfloat16))
        cross_spec = cross_spec.astype(jnp.float32)
        spectrum_full = cross_spec[:, :SEG] + 1j * cross_spec[:, SEG:]
        spectrum_full = jnp.pad(spectrum_full, ((0, 0), (0, 1)))
        lagged = jnp.fft.irfft(spectrum_full, n=2 * SEG, axis=1) * (2 * SEG) / math.sqrt(SEG)
        lagged = jnp.concatenate([lagged[:, 2 * SEG - SEG // 2:], lagged[:, :SEG // 2]], axis=1)
        live_mask = jnp.arange(PAIR_CAP, dtype=jnp.int32) < live_count
        return jnp.where(live_mask[:, None], lagged, 0.0).astype(jnp.float32)
    result = lax.map(one_owner, (firsts, seconds, pair_count))
    return result.reshape(OWNERS * PAIR_CAP, SEG)
```

```python
import functools
import math

import jax
import jax.numpy as jnp
import ml_dtypes
import numpy as np
from jax import lax
from jax.experimental import pallas as pl
from jax.experimental.pallas import tpu as pltpu
from jax.sharding import PartitionSpec as P

NB = 100
SEG = 512
SEGS = 12
TILE = 128
PER_SEG = SEG // TILE
KB = SEG // 128
ROWS = 2 * SEGS * KB
PAIR_BLOCK = 256
UNROLL = 8


def forward_table():
    phase = np.outer(np.arange(SEG), np.arange(SEG)) % (2 * SEG) * (math.pi / SEG)
    table = np.concatenate([np.cos(phase), -np.sin(phase)], axis=1) / math.sqrt(SEG)
    return table.astype(np.float32).astype(ml_dtypes.bfloat16)


def inverse_table():
    phase = np.outer(np.arange(SEG), np.arange(SEG) - SEG // 2) % (2 * SEG) * (math.pi / SEG)
    weights = np.where(np.arange(SEG)[:, None] == 0, 1.0, 2.0) / math.sqrt(SEG) / SEGS
    table = np.concatenate([weights * np.cos(phase), -weights * np.sin(phase)], axis=0)
    return table.astype(np.float32).astype(ml_dtypes.bfloat16)


def whiten_block(rows, fwd, lhs, spec, rowed, white, base):
    count = rows.shape[1]
    for s in range(SEGS):
        parts = [rows[s * PER_SEG + q].astype(jnp.float32) for q in range(PER_SEG)]
        squares = sum(part * part for part in parts)
        gain = lax.rsqrt(jnp.sum(squares, axis=1, keepdims=True) / SEG + 1e-05)
        for q in range(PER_SEG):
            lhs[s * count:(s + 1) * count, q * TILE:(q + 1) * TILE] = (parts[q] * gain).astype(jnp.bfloat16)
    total = SEGS * count
    for n in range(2 * SEG // 256):
        cols = slice(n * 256, (n + 1) * 256)
        spec[:total, cols] = jnp.dot(lhs[:total], fwd[:, cols], preferred_element_type=jnp.float32)
    for k in range(KB):
        re_cols = slice(k * 128, (k + 1) * 128)
        im_cols = slice(SEG + k * 128, SEG + (k + 1) * 128)
        level = jnp.zeros((count, 128), jnp.float32)
        for s in range(SEGS):
            re = spec[s * count:(s + 1) * count, re_cols]
            im = spec[s * count:(s + 1) * count, im_cols]
            level = level + (re * re + im * im)
        gain = lax.rsqrt(level / SEGS + 0.5)
        for s in range(SEGS):
            row = s * KB + k
            rowed[pl.ds(row, count, stride=ROWS), :] = spec[s * count:(s + 1) * count, re_cols] * gain
            rowed[pl.ds(row + ROWS // 2, count, stride=ROWS), :] = spec[s * count:(s + 1) * count, im_cols] * gain

    def pack(c, carry):
        start = pl.multiple_of(c * ROWS, ROWS)
        white[base + c] = rowed[pl.ds(start, ROWS), :].astype(jnp.bfloat16)
        return carry

    lax.fori_loop(0, count, pack, 0, unroll=4)


def fold(tile):
    wide = tile.astype(jnp.float32)
    return wide[:8] + wide[8:]


def correlate_kernel(pairs_ref, count_ref, own, near, far, fwd, inv, out, lhs, spec, rowed, white, cross):
    channels = own.shape[1]
    offset = (lax.axis_index("tm") * lax.axis_size("pairs") + lax.axis_index("pairs")) * channels
    base = 0
    for rows in (own, near, far):
        whiten_block(rows, fwd, lhs, spec, rowed, white, base)
        base += rows.shape[1]
    low_half = lax.broadcasted_iota(jnp.int32, (8, 128), 0) < 4

    def one_pair(slot, place):
        left = white[pairs_ref[0, slot] - offset]
        right = white[pairs_ref[1, slot] - offset]
        half = ROWS // 2
        lr, li, rr, ri = left[:half], left[half:], right[:half], right[half:]
        re = lr * rr + li * ri
        im = li * rr - lr * ri
        re = fold(re[:16] + re[16:32] + re[32:])
        im = fold(im[:16] + im[16:32] + im[32:])
        straight = jnp.where(low_half, re, im)
        crossed = jnp.where(low_half, im, re)
        cross[pl.ds(pl.multiple_of(place * 8, 8), 8), :] = straight + pltpu.roll(crossed, 4, 0)

    def one_block(block, carry):
        start = pl.multiple_of(block * PAIR_BLOCK, PAIR_BLOCK)

        def some_pairs(step, inner):
            for u in range(UNROLL):
                place = step * UNROLL + u
                one_pair(start + place, place)
            return inner

        lax.fori_loop(0, PAIR_BLOCK // UNROLL, some_pairs, 0)
        pieces = [cross[pl.ds(r, PAIR_BLOCK, stride=8), :].astype(jnp.bfloat16) for r in range(8)]
        lagged = jnp.dot(jnp.concatenate(pieces, axis=1), inv[...], preferred_element_type=jnp.float32)
        slots = start + lax.broadcasted_iota(jnp.int32, (PAIR_BLOCK, SEG), 0)
        out[pl.ds(start, PAIR_BLOCK), :] = jnp.where(slots < count_ref[0], lagged, 0.0)
        return carry

    lax.fori_loop(0, out.shape[0] // PAIR_BLOCK, one_block, 0)


def correlate(pair_list, pair_count, own, near, far):
    channels = own.shape[1]
    reach = channels + near.shape[1] + far.shape[1]
    capacity = pair_list.shape[1]
    smem = pl.BlockSpec(memory_space=pltpu.SMEM)
    vmem = pl.BlockSpec(memory_space=pltpu.VMEM)
    return pl.pallas_call(
        correlate_kernel,
        out_shape=jax.ShapeDtypeStruct((capacity, SEG), jnp.float32),
        in_specs=[smem, smem, vmem, vmem, vmem, vmem, vmem],
        out_specs=vmem,
        scratch_shapes=[
            pltpu.VMEM((SEGS * channels, SEG), jnp.bfloat16),
            pltpu.VMEM((SEGS * channels, 2 * SEG), jnp.float32),
            pltpu.VMEM((channels * ROWS, 128), jnp.float32),
            pltpu.VMEM((reach, ROWS, 128), jnp.bfloat16),
            pltpu.VMEM((PAIR_BLOCK * 8, 128), jnp.float32),
        ],
        compiler_params=pltpu.CompilerParams(vmem_limit_bytes=48 * 1024 * 1024),
        name="correlate",
    )(pair_list, pair_count, own, near, far, jnp.asarray(forward_table()), jnp.asarray(inverse_table()))


def from_behind(block, axis, distance):
    devices = range(lax.axis_size(axis))
    route = [(i - distance, i) for i in devices if i - distance in devices]
    return lax.ppermute(block, axis, route)


def per_device(panels, pair_list, pair_count):
    relaid = lax.all_to_all(panels, "tm", split_axis=1, concat_axis=0, tiled=True)
    own = relaid[:, 0]
    channels = own.shape[1]
    far_count = -(-(NB - channels) // 16) * 16
    near = from_behind(own, "pairs", -1)
    far = from_behind(own[:, :far_count], "pairs", -2)
    return correlate(pair_list, pair_count, own, near, far)


def solution(mesh):
    return jax.shard_map(
        per_device,
        mesh=mesh,
        in_specs=(P("tm", None, "pairs", None), P(None, ("tm", "pairs")), P(("tm", "pairs"))),
        out_specs=P(("tm", "pairs"), None),
        check_vma=False,
    )
```

```python
import math

import jax
import jax.numpy as jnp
import ml_dtypes
import numpy as np
from jax import lax
from jax.experimental import pallas as pl
from jax.experimental.pallas import tpu as pltpu
from jax.sharding import PartitionSpec as P

CH_DEV = 64
NB = 100
SEG = 512
SEGS = 12
TILE = 128
PER_SEG = SEG // TILE
KB = SEG // 128
ROWS = 2 * SEGS * KB
PAIR_BLOCK = 256
UNROLL = 8


def forward_table():
    phase = np.outer(np.arange(SEG), np.arange(SEG)) % (2 * SEG) * (math.pi / SEG)
    table = np.concatenate([np.cos(phase), -np.sin(phase)], axis=1) / math.sqrt(SEG)
    return table.astype(np.float32).astype(ml_dtypes.bfloat16)


def inverse_table():
    phase = np.outer(np.arange(SEG), np.arange(SEG) - SEG // 2) % (2 * SEG) * (math.pi / SEG)
    weights = np.where(np.arange(SEG)[:, None] == 0, 1.0, 2.0) / math.sqrt(SEG) / SEGS
    table = np.concatenate([weights * np.cos(phase), -weights * np.sin(phase)], axis=0)
    return table.astype(np.float32).astype(ml_dtypes.bfloat16)


def transform_tiles(rows, fwd, lhs, spec, first_seg, seg_count):
    count = rows.shape[1]
    for s in range(seg_count):
        tiles = [rows[(first_seg + s) * PER_SEG + q].astype(jnp.float32) for q in range(PER_SEG)]
        squares = sum(tile * tile for tile in tiles)
        gain = lax.rsqrt(jnp.sum(squares, axis=1, keepdims=True) / SEG + 1e-05)
        for q in range(PER_SEG):
            lhs[s * count:(s + 1) * count, q * TILE:(q + 1) * TILE] = (tiles[q] * gain).astype(jnp.bfloat16)
    total = seg_count * count
    start = first_seg * count
    for n in range(2 * SEG // 256):
        cols = slice(n * 256, (n + 1) * 256)
        spec[start:start + total, cols] = jnp.dot(lhs[:total], fwd[:, cols], preferred_element_type=jnp.float32)


def whiten_block(count, spec, rowed, white, base):
    for k in range(KB):
        re_cols = slice(k * 128, (k + 1) * 128)
        im_cols = slice(SEG + k * 128, SEG + (k + 1) * 128)
        level = jnp.zeros((count, 128), jnp.float32)
        for s in range(SEGS):
            re = spec[s * count:(s + 1) * count, re_cols]
            im = spec[s * count:(s + 1) * count, im_cols]
            level = level + (re * re + im * im)
        gain = lax.rsqrt(level / SEGS + 0.5)
        for s in range(SEGS):
            row = s * KB + k
            rowed[pl.ds(row, count, stride=ROWS), :] = spec[s * count:(s + 1) * count, re_cols] * gain
            rowed[pl.ds(row + ROWS // 2, count, stride=ROWS), :] = spec[s * count:(s + 1) * count, im_cols] * gain

    def pack(c, carry):
        start = pl.multiple_of(c * ROWS, ROWS)
        white[base + c] = rowed[pl.ds(start, ROWS), :].astype(jnp.bfloat16)
        return carry

    lax.fori_loop(0, count, pack, 0, unroll=4)


def gather_kernel(panels, fwd, white, own, near, far, lhs, spec_own, spec_near, spec_far, rowed,
                  local_sem, own_send, halo_send, pass_near_send, pass_far_send, own_recv, near_recv, far_recv):
    section = lax.axis_index("tm")
    place = lax.axis_index("pairs")
    sections, places = lax.axis_size("tm"), lax.axis_size("pairs")
    local_tiles = panels.shape[0]
    channels, far_count = own.shape[1], far.shape[1]
    odd = lax.rem(place, 2) == 1
    even = lax.rem(place, 2) == 0
    has_below = place >= 2
    has_above = place < places - 2
    below = place - 2 + lax.rem(place + 1, 2)
    sibling = place - 1 + 2 * lax.rem(place + 1, 2)

    barrier = pltpu.get_barrier_semaphore()

    def greet(other_section, other_place):
        pl.semaphore_signal(barrier, inc=1, device_id=(other_section, other_place),
                            device_id_type=pl.DeviceIdType.MESH)

    for d in range(1, sections):
        greet(lax.rem(section + d, sections), place)

    @pl.when(odd & has_above)
    def _():
        for d in range(sections):
            greet(lax.rem(section + d, sections), place + 1)
            greet(lax.rem(section + d, sections), place + 2)

    @pl.when(even)
    def _():
        greet(section, sibling)

    targets = sections - 1 + sections * has_below.astype(jnp.int32) + lax.rem(place, 2)
    pl.semaphore_wait(barrier, targets)

    mine = pl.ds(section * local_tiles, local_tiles)

    def tiles_of(t):
        return pl.ds(t * local_tiles, local_tiles)

    def own_copy(d):
        to = lax.rem(section + d, sections)
        return pltpu.make_async_remote_copy(
            src_ref=panels.at[:, to], dst_ref=own.at[mine], send_sem=own_send.at[d],
            recv_sem=own_recv.at[section], device_id=(to, place), device_id_type=pl.DeviceIdType.MESH)

    def near_copy(d):
        to = lax.rem(section + d, sections)
        return pltpu.make_async_remote_copy(
            src_ref=panels.at[:, to], dst_ref=near.at[mine], send_sem=halo_send.at[d],
            recv_sem=near_recv.at[section], device_id=(to, below), device_id_type=pl.DeviceIdType.MESH)

    def far_copy(d):
        to = lax.rem(section + d, sections)
        return pltpu.make_async_remote_copy(
            src_ref=panels.at[:, to, pl.ds(0, far_count)], dst_ref=far.at[mine], send_sem=halo_send.at[d],
            recv_sem=far_recv.at[section], device_id=(to, below), device_id_type=pl.DeviceIdType.MESH)

    def pass_near(t):
        return pltpu.make_async_remote_copy(
            src_ref=own.at[tiles_of(t)], dst_ref=near.at[tiles_of(t)], send_sem=pass_near_send.at[t],
            recv_sem=near_recv.at[t], device_id=(section, sibling), device_id_type=pl.DeviceIdType.MESH)

    def pass_far(t):
        return pltpu.make_async_remote_copy(
            src_ref=near.at[tiles_of(t), pl.ds(0, far_count)], dst_ref=far.at[tiles_of(t)],
            send_sem=pass_far_send.at[t], recv_sem=far_recv.at[t], device_id=(section, sibling),
            device_id_type=pl.DeviceIdType.MESH)

    def arrived(buffer, sems, t):
        pltpu.make_async_copy(buffer.at[tiles_of(t)], buffer.at[tiles_of(t)], sems.at[t]).wait()

    keep = pltpu.make_async_copy(panels.at[:, section], own.at[mine], own_recv.at[section])
    keep.start()
    for d in range(sections):
        @pl.when(has_below & even)
        def _():
            near_copy(d).start()

        @pl.when(has_below & odd)
        def _():
            far_copy(d).start()

        if d > 0:
            own_copy(d).start()

    group = PER_SEG // math.gcd(PER_SEG, local_tiles)
    segs = group * local_tiles // PER_SEG

    def block_in(buffer, sems, spec, onward, onward_if):
        for g in range(sections // group):
            for t in range(g * group, (g + 1) * group):
                arrived(buffer, sems, t)
                if onward is not None:
                    @pl.when(onward_if)
                    def _():
                        onward(t).start()
            transform_tiles(buffer, fwd, lhs, spec, g * segs, segs)

    block_in(own, own_recv, spec_own, pass_near, odd)
    whiten_block(channels, spec_own, rowed, white, 0)

    @pl.when(even | has_above)
    def _():
        block_in(near, near_recv, spec_near, pass_far, odd)
        whiten_block(channels, spec_near, rowed, white, channels)

    @pl.when(has_above)
    def _():
        block_in(far, far_recv, spec_far, None, None)
        whiten_block(far_count, spec_far, rowed, white, 2 * channels)

    for d in range(sections):
        @pl.when(has_below & even)
        def _():
            near_copy(d).wait_send()

        @pl.when(has_below & odd)
        def _():
            far_copy(d).wait_send()

        if d > 0:
            own_copy(d).wait_send()

    @pl.when(odd)
    def _():
        for t in range(sections):
            pass_near(t).wait_send()

    @pl.when(odd & has_above)
    def _():
        for t in range(sections):
            pass_far(t).wait_send()


def gather(panels):
    local_tiles, sections, channels, _ = panels.shape
    tiles = local_tiles * sections
    far_count = -(-(NB - channels) // 16) * 16
    reach = 2 * channels + far_count
    dma = pltpu.SemaphoreType.DMA((sections,))
    return pl.pallas_call(
        gather_kernel,
        out_shape=jax.ShapeDtypeStruct((reach, ROWS, 128), jnp.bfloat16),
        in_specs=[pl.BlockSpec(memory_space=pl.ANY), pl.BlockSpec(memory_space=pltpu.VMEM)],
        out_specs=pl.BlockSpec(memory_space=pltpu.VMEM),
        scratch_shapes=[
            pltpu.VMEM((tiles, channels, TILE), jnp.bfloat16),
            pltpu.VMEM((tiles, channels, TILE), jnp.bfloat16),
            pltpu.VMEM((tiles, far_count, TILE), jnp.bfloat16),
            pltpu.VMEM((SEGS * channels, SEG), jnp.bfloat16),
            pltpu.VMEM((SEGS * channels, 2 * SEG), jnp.float32),
            pltpu.VMEM((SEGS * channels, 2 * SEG), jnp.float32),
            pltpu.VMEM((SEGS * far_count, 2 * SEG), jnp.float32),
            pltpu.VMEM((channels * ROWS, 128), jnp.float32),
            pltpu.SemaphoreType.DMA, dma, dma, dma, dma, dma, dma, dma,
        ],
        compiler_params=pltpu.CompilerParams(
            vmem_limit_bytes=40 * 1024 * 1024, collective_id=0, has_side_effects=True),
        name="gather",
    )(panels, jnp.asarray(forward_table()))


def fold(tile):
    wide = tile.astype(jnp.float32)
    return wide[:8] + wide[8:]


def correlate_kernel(pairs_ref, count_ref, white, inv, out, cross):
    owner = lax.axis_index("tm") * lax.axis_size("pairs") + lax.axis_index("pairs")
    offset = owner * CH_DEV
    low_half = lax.broadcasted_iota(jnp.int32, (8, 128), 0) < 4

    def one_pair(slot, place):
        left = white[pairs_ref[0, slot] - offset]
        right = white[pairs_ref[1, slot] - offset]
        half = ROWS // 2
        lr, li, rr, ri = left[:half], left[half:], right[:half], right[half:]
        re = lr * rr + li * ri
        im = li * rr - lr * ri
        re = fold(re[:16] + re[16:32] + re[32:])
        im = fold(im[:16] + im[16:32] + im[32:])
        straight = jnp.where(low_half, re, im)
        crossed = jnp.where(low_half, im, re)
        cross[pl.ds(pl.multiple_of(place * 8, 8), 8), :] = straight + pltpu.roll(crossed, 4, 0)

    def one_block(block, carry):
        start = pl.multiple_of(block * PAIR_BLOCK, PAIR_BLOCK)

        def some_pairs(step, inner):
            for u in range(UNROLL):
                place = step * UNROLL + u
                one_pair(start + place, place)
            return inner

        lax.fori_loop(0, PAIR_BLOCK // UNROLL, some_pairs, 0)
        pieces = [cross[pl.ds(r, PAIR_BLOCK, stride=8), :].astype(jnp.bfloat16) for r in range(8)]
        lagged = jnp.dot(jnp.concatenate(pieces, axis=1), inv[...], preferred_element_type=jnp.float32)
        slots = start + lax.broadcasted_iota(jnp.int32, (PAIR_BLOCK, SEG), 0)
        out[pl.ds(start, PAIR_BLOCK), :] = jnp.where(slots < count_ref[0], lagged, 0.0)
        return carry

    lax.fori_loop(0, out.shape[0] // PAIR_BLOCK, one_block, 0)


def correlate(pair_list, pair_count, white):
    capacity = pair_list.shape[1]
    smem = pl.BlockSpec(memory_space=pltpu.SMEM)
    vmem = pl.BlockSpec(memory_space=pltpu.VMEM)
    return pl.pallas_call(
        correlate_kernel,
        out_shape=jax.ShapeDtypeStruct((capacity, SEG), jnp.float32),
        in_specs=[smem, smem, vmem, vmem],
        out_specs=vmem,
        scratch_shapes=[pltpu.VMEM((PAIR_BLOCK * 8, 128), jnp.float32)],
        compiler_params=pltpu.CompilerParams(vmem_limit_bytes=24 * 1024 * 1024),
        name="correlate",
    )(pair_list, pair_count, white, jnp.asarray(inverse_table()))


def per_device(panels, pair_list, pair_count):
    return correlate(pair_list, pair_count, gather(panels))


def solution(mesh):
    return jax.shard_map(
        per_device,
        mesh=mesh,
        in_specs=(P("tm", None, "pairs", None), P(None, ("tm", "pairs")), P(("tm", "pairs"))),
        out_specs=P(("tm", "pairs"), None),
        check_vma=False,
    )
```

```python
import math

import jax
import jax.numpy as jnp
import ml_dtypes
import numpy as np
from jax import lax
from jax.experimental import pallas as pl
from jax.experimental.pallas import tpu as pltpu
from jax.sharding import PartitionSpec as P

CH_DEV = 64
NB = 100
SEG = 512
SEGS = 12
TILE = 128
PER_SEG = SEG // TILE
KB = SEG // 128
ROWS = 2 * SEGS * KB
PAIR_BLOCK = 256
ROW_PITCH = ROWS + 1
PAIR_PITCH = 9
UNROLL = 8


def forward_table():
    phase = np.outer(np.arange(SEG), np.arange(SEG)) % (2 * SEG) * (math.pi / SEG)
    table = np.concatenate([np.cos(phase), -np.sin(phase)], axis=1) / math.sqrt(SEG)
    return table.astype(np.float32).astype(ml_dtypes.bfloat16)


def inverse_table():
    phase = np.outer(np.arange(SEG), np.arange(SEG) - SEG // 2) % (2 * SEG) * (math.pi / SEG)
    weights = np.where(np.arange(SEG)[:, None] == 0, 1.0, 2.0) / math.sqrt(SEG) / SEGS
    table = np.concatenate([weights * np.cos(phase), -weights * np.sin(phase)], axis=0)
    return table.astype(np.float32).astype(ml_dtypes.bfloat16)


def transform_tiles(rows, fwd, lhs, spec, first_seg, seg_count):
    count = rows.shape[1]
    for s in range(seg_count):
        tiles = [rows[(first_seg + s) * PER_SEG + q].astype(jnp.float32) for q in range(PER_SEG)]
        squares = sum(tile * tile for tile in tiles)
        gain = lax.rsqrt(jnp.sum(squares, axis=1, keepdims=True) / SEG + 1e-05)
        for q in range(PER_SEG):
            lhs[s * count:(s + 1) * count, q * TILE:(q + 1) * TILE] = (tiles[q] * gain).astype(jnp.bfloat16)
    total = seg_count * count
    start = first_seg * count
    for n in range(2 * SEG // 256):
        cols = slice(n * 256, (n + 1) * 256)
        spec[start:start + total, cols] = jnp.dot(lhs[:total], fwd[:, cols], preferred_element_type=jnp.float32)


def whiten_block(count, spec, rowed, white, base):
    for k in range(KB):
        re_cols = slice(k * 128, (k + 1) * 128)
        im_cols = slice(SEG + k * 128, SEG + (k + 1) * 128)
        level = jnp.zeros((count, 128), jnp.float32)
        for s in range(SEGS):
            re = spec[s * count:(s + 1) * count, re_cols]
            im = spec[s * count:(s + 1) * count, im_cols]
            level = level + (re * re + im * im)
        gain = lax.rsqrt(level / SEGS + 0.5)
        for s in range(SEGS):
            row = s * KB + k
            rowed[pl.ds(row, count, stride=ROW_PITCH), :] = spec[s * count:(s + 1) * count, re_cols] * gain
            rowed[pl.ds(row + ROWS // 2, count, stride=ROW_PITCH), :] = spec[s * count:(s + 1) * count, im_cols] * gain

    def pack(c, carry):
        white[base + c] = rowed[pl.ds(c * ROW_PITCH, ROWS), :].astype(jnp.bfloat16)
        return carry

    lax.fori_loop(0, count, pack, 0, unroll=4)


def flipped(index, mask):
    bit = 1
    while bit <= mask:
        if mask & bit:
            index = index + bit * (1 - 2 * lax.rem(index // bit, 2))
        bit *= 2
    return index


def gather_kernel(panels, fwd_hbm, white, fwd, own, near, far, lhs, spec_own, spec_near, spec_far, rowed,
                  table_sem, own_send, below_send, near_send, far_send, own_recv, near_recv, far_recv):
    section = lax.axis_index("tm")
    place = lax.axis_index("pairs")
    sections, places = lax.axis_size("tm"), lax.axis_size("pairs")
    local_tiles = panels.shape[0]
    channels, far_count = own.shape[1], far.shape[1]
    group = PER_SEG // math.gcd(PER_SEG, local_tiles)
    segs = local_tiles // PER_SEG
    odd = lax.rem(place, 2) == 1
    even = lax.rem(place, 2) == 0
    has_below = place >= 2
    has_above = place < places - 2
    below = place - 2 + lax.rem(place + 1, 2)
    sibling = place - 1 + 2 * lax.rem(place + 1, 2)

    table_copy = pltpu.make_async_copy(fwd_hbm, fwd, table_sem)
    table_copy.start()
    barrier = pltpu.get_barrier_semaphore()

    def greet(other_section, other_place):
        pl.semaphore_signal(barrier, inc=1, device_id=(other_section, other_place),
                            device_id_type=pl.DeviceIdType.MESH)

    for d in range(1, sections):
        greet(flipped(section, d), place)

    @pl.when(odd & has_above)
    def _():
        greet(section, place + 1)
        greet(section, place + 2)

    @pl.when(even)
    def _():
        greet(section, sibling)

    targets = sections - 1 + has_below.astype(jnp.int32) + lax.rem(place, 2)
    pl.semaphore_wait(barrier, targets)

    def slot(d):
        return d if group == 1 else flipped(section, d)

    def part(buffer, d):
        return buffer.at[pl.ds(slot(d) * local_tiles, local_tiles)]

    def remote(src, dst, send, recv, device):
        return pltpu.make_async_remote_copy(src_ref=src, dst_ref=dst, send_sem=send, recv_sem=recv,
                                            device_id=device, device_id_type=pl.DeviceIdType.MESH)

    def own_copy(d):
        to = flipped(section, d)
        at = d if group == 1 else section
        return remote(panels.at[:, to], own.at[pl.ds(at * local_tiles, local_tiles)], own_send.at[d],
                      own_recv.at[d], (to, place))

    def held(d):
        return panels.at[:, section] if d == 0 else part(own, d)

    def near_below(d):
        return remote(held(d), part(near, d), below_send.at[d], near_recv.at[d], (section, below))

    def far_below(d):
        return remote(held(d).at[:, pl.ds(0, far_count)], part(far, d), below_send.at[d], far_recv.at[d],
                      (section, below))

    def near_aside(d):
        return remote(held(d), part(near, d), near_send.at[d], near_recv.at[d], (section, sibling))

    def far_aside(d):
        return remote(part(near, d).at[:, pl.ds(0, far_count)], part(far, d), far_send.at[d], far_recv.at[d],
                      (section, sibling))

    def arrived(buffer, sems, d):
        pltpu.make_async_copy(part(buffer, d), part(buffer, d), sems.at[d]).wait()

    def onward(d):
        @pl.when(has_below & even)
        def _():
            near_below(d).start()

        @pl.when(has_below & odd)
        def _():
            far_below(d).start()

        @pl.when(odd)
        def _():
            near_aside(d).start()

    def transform(buffer, spec, d):
        if group == 1:
            transform_tiles(buffer, fwd, lhs, spec, d * segs, segs)
        elif d == sections - 1:
            transform_tiles(buffer, fwd, lhs, spec, 0, SEGS)

    for d in range(1, sections):
        own_copy(d).start()
    keep = pltpu.make_async_copy(panels.at[:, section], part(own, 0), own_recv.at[0])
    keep.start()
    onward(0)
    table_copy.wait()
    keep.wait()
    for d in range(1, sections):
        transform(own, spec_own, d - 1)
        arrived(own, own_recv, d)
        onward(d)
    transform(own, spec_own, sections - 1)
    whiten_block(channels, spec_own, rowed, white, 0)

    def take_near(d):
        arrived(near, near_recv, d)

        @pl.when(odd)
        def _():
            far_aside(d).start()

        transform(near, spec_near, d)

    @pl.when(has_above)
    def _():
        for d in range(sections):
            take_near(d)
            arrived(far, far_recv, d)
            transform(far, spec_far, d)
        whiten_block(channels, spec_near, rowed, white, channels)
        whiten_block(far_count, spec_far, rowed, white, 2 * channels)

    @pl.when((place >= places - 2) & even)
    def _():
        for d in range(sections):
            arrived(near, near_recv, d)
            transform(near, spec_near, d)
        whiten_block(channels, spec_near, rowed, white, channels)

    for d in range(sections):
        @pl.when(has_below & even)
        def _():
            near_below(d).wait_send()

        @pl.when(has_below & odd)
        def _():
            far_below(d).wait_send()

        @pl.when(odd)
        def _():
            near_aside(d).wait_send()

        @pl.when(odd & has_above)
        def _():
            far_aside(d).wait_send()

        if d > 0:
            own_copy(d).wait_send()


def gather(panels):
    local_tiles, sections, channels, _ = panels.shape
    tiles = local_tiles * sections
    far_count = -(-(NB - channels) // 16) * 16
    reach = 2 * channels + far_count
    dma = pltpu.SemaphoreType.DMA((sections,))
    return pl.pallas_call(
        gather_kernel,
        out_shape=jax.ShapeDtypeStruct((reach, ROWS, 128), jnp.bfloat16),
        in_specs=[pl.BlockSpec(memory_space=pltpu.HBM)] * 2,
        out_specs=pl.BlockSpec(memory_space=pltpu.VMEM),
        scratch_shapes=[
            pltpu.VMEM((SEG, 2 * SEG), jnp.bfloat16),
            pltpu.VMEM((tiles, channels, TILE), jnp.bfloat16),
            pltpu.VMEM((tiles, channels, TILE), jnp.bfloat16),
            pltpu.VMEM((tiles, far_count, TILE), jnp.bfloat16),
            pltpu.VMEM((SEGS * channels, SEG), jnp.bfloat16),
            pltpu.VMEM((SEGS * channels, 2 * SEG), jnp.float32),
            pltpu.VMEM((SEGS * channels, 2 * SEG), jnp.float32),
            pltpu.VMEM((SEGS * far_count, 2 * SEG), jnp.float32),
            pltpu.VMEM(((channels + 1) * ROW_PITCH, 128), jnp.float32),
            pltpu.SemaphoreType.DMA, dma, dma, dma, dma, dma, dma, dma,
        ],
        compiler_params=pltpu.CompilerParams(
            vmem_limit_bytes=40 * 1024 * 1024, collective_id=0, has_side_effects=True),
        name="gather",
    )(panels, jnp.asarray(forward_table()))


def fold(tile):
    wide = tile.astype(jnp.float32)
    return wide[:8] + wide[8:]


def correlate_kernel(pairs_ref, count_ref, white, inv, out, cross):
    owner = lax.axis_index("tm") * lax.axis_size("pairs") + lax.axis_index("pairs")
    offset = owner * CH_DEV
    low_half = lax.broadcasted_iota(jnp.int32, (8, 128), 0) < 4

    def one_pair(slot, place):
        left = white[pairs_ref[0, slot] - offset]
        right = white[pairs_ref[1, slot] - offset]
        half = ROWS // 2
        lr, li, rr, ri = left[:half], left[half:], right[:half], right[half:]
        re = lr * rr + li * ri
        im = li * rr - lr * ri
        re = fold(re[:16] + re[16:32] + re[32:])
        im = fold(im[:16] + im[16:32] + im[32:])
        straight = jnp.where(low_half, re, im)
        crossed = jnp.where(low_half, im, re)
        cross[pl.ds(place * PAIR_PITCH, 8), :] = straight + pltpu.roll(crossed, 4, 0)

    def one_block(block, carry):
        start = pl.multiple_of(block * PAIR_BLOCK, PAIR_BLOCK)

        def some_pairs(step, inner):
            for u in range(UNROLL):
                place = step * UNROLL + u
                one_pair(start + place, place)
            return inner

        lax.fori_loop(0, PAIR_BLOCK // UNROLL, some_pairs, 0)
        pieces = [cross[pl.ds(r, PAIR_BLOCK, stride=PAIR_PITCH), :].astype(jnp.bfloat16) for r in range(8)]
        lagged = jnp.dot(jnp.concatenate(pieces, axis=1), inv[...], preferred_element_type=jnp.float32)
        slots = start + lax.broadcasted_iota(jnp.int32, (PAIR_BLOCK, SEG), 0)
        out[pl.ds(start, PAIR_BLOCK), :] = jnp.where(slots < count_ref[0], lagged, 0.0)
        return carry

    lax.fori_loop(0, out.shape[0] // PAIR_BLOCK, one_block, 0)


def correlate(pair_list, pair_count, white):
    capacity = pair_list.shape[1]
    smem = pl.BlockSpec(memory_space=pltpu.SMEM)
    vmem = pl.BlockSpec(memory_space=pltpu.VMEM)
    return pl.pallas_call(
        correlate_kernel,
        out_shape=jax.ShapeDtypeStruct((capacity, SEG), jnp.float32),
        in_specs=[smem, smem, vmem, vmem],
        out_specs=vmem,
        scratch_shapes=[pltpu.VMEM(((PAIR_BLOCK + 1) * PAIR_PITCH, 128), jnp.float32)],
        compiler_params=pltpu.CompilerParams(vmem_limit_bytes=24 * 1024 * 1024),
        name="correlate",
    )(pair_list, pair_count, white, jnp.asarray(inverse_table()))


def per_device(panels, pair_list, pair_count):
    return correlate(pair_list, pair_count, gather(panels))


def solution(mesh):
    return jax.shard_map(
        per_device,
        mesh=mesh,
        in_specs=(P("tm", None, "pairs", None), P(None, ("tm", "pairs")), P(("tm", "pairs"))),
        out_specs=P(("tm", "pairs"), None),
        check_vma=False,
    )
```

```python
import math

import jax
import jax.numpy as jnp
import ml_dtypes
import numpy as np
from jax import lax
from jax.experimental import pallas as pl
from jax.experimental.pallas import tpu as pltpu
from jax.sharding import PartitionSpec as P

CH_DEV = 64
NB = 100
SEG = 512
SEGS = 12
TILE = 128
PER_SEG = SEG // TILE
KB = SEG // 128
ROWS = 2 * SEGS * KB
PAIR_BLOCK = 256
ROW_PITCH = ROWS + 1
PAIR_PITCH = 9
VMEM_BYTES = 40 * 1024 * 1024
UNROLL = 8


def forward_table():
    phase = np.outer(np.arange(SEG), np.arange(SEG)) % (2 * SEG) * (math.pi / SEG)
    table = np.concatenate([np.cos(phase), -np.sin(phase)], axis=1) / math.sqrt(SEG)
    return table.astype(np.float32).astype(ml_dtypes.bfloat16)


def inverse_table():
    phase = np.outer(np.arange(SEG), np.arange(SEG) - SEG // 2) % (2 * SEG) * (math.pi / SEG)
    weights = np.where(np.arange(SEG)[:, None] == 0, 1.0, 2.0) / math.sqrt(SEG) / SEGS
    table = np.concatenate([weights * np.cos(phase), -weights * np.sin(phase)], axis=0)
    return table.astype(np.float32).astype(ml_dtypes.bfloat16)


def transform_tiles(rows, fwd, lhs, rowed, first_seg, seg_count):
    count = rows.shape[1]
    for s in range(seg_count):
        tiles = [rows[(first_seg + s) * PER_SEG + q].astype(jnp.float32) for q in range(PER_SEG)]
        squares = sum(tile * tile for tile in tiles)
        gain = lax.rsqrt(jnp.sum(squares, axis=1, keepdims=True) / SEG + 1e-05)
        for q in range(PER_SEG):
            lhs[s * count:(s + 1) * count, q * TILE:(q + 1) * TILE] = (tiles[q] * gain).astype(jnp.bfloat16)
    for n in range(2 * SEG // 256):
        spectrum = jnp.dot(lhs[:seg_count * count], fwd[:, n * 256:(n + 1) * 256],
                           preferred_element_type=jnp.float32)
        for s in range(seg_count):
            for h in range(2):
                part, k = divmod(2 * n + h, KB)
                row = part * (ROWS // 2) + (first_seg + s) * KB + k
                rowed[pl.ds(row, count, stride=ROW_PITCH), :] = spectrum[s * count:(s + 1) * count,
                                                                         h * 128:(h + 1) * 128]


def whiten_block(count, rowed, white, base):
    def one_channel(c, carry):
        rows = rowed[pl.ds(c * ROW_PITCH, ROWS), :]
        tiles = [rows[t * 8:(t + 1) * 8] for t in range(ROWS // 8)]
        squares = [tile * tile for tile in tiles]
        while len(squares) > 1:
            odd_one = squares[len(squares) // 2 * 2:]
            squares = [squares[t] + squares[t + 1] for t in range(0, len(squares) - 1, 2)] + odd_one
        level = squares[0] + pltpu.roll(squares[0], 4, 0)
        gain = lax.rsqrt(level / SEGS + 0.5)
        white[base + c] = jnp.concatenate([tile * gain for tile in tiles], axis=0).astype(jnp.bfloat16)
        return carry

    lax.fori_loop(0, count, one_channel, 0, unroll=4)


def flipped(index, mask):
    bit = 1
    while bit <= mask:
        if mask & bit:
            index = index + bit * (1 - 2 * lax.rem(index // bit, 2))
        bit *= 2
    return index


def gather_kernel(panels, fwd_hbm, white, fwd, own, near, far, lhs, row_own, row_near, row_far,
                  table_sem, own_send, below_send, near_send, far_send, own_recv, near_recv, far_recv):
    section = lax.axis_index("tm")
    place = lax.axis_index("pairs")
    sections, places = lax.axis_size("tm"), lax.axis_size("pairs")
    local_tiles = panels.shape[0]
    channels, far_count = own.shape[1], far.shape[1]
    group = PER_SEG // math.gcd(PER_SEG, local_tiles)
    segs = local_tiles // PER_SEG
    odd = lax.rem(place, 2) == 1
    even = lax.rem(place, 2) == 0
    has_below = place >= 2
    has_above = place < places - 2
    below = place - 2 + lax.rem(place + 1, 2)
    sibling = place - 1 + 2 * lax.rem(place + 1, 2)

    table_copy = pltpu.make_async_copy(fwd_hbm, fwd, table_sem)
    table_copy.start()
    barrier = pltpu.get_barrier_semaphore()

    def greet(other_section, other_place):
        pl.semaphore_signal(barrier, inc=1, device_id=(other_section, other_place),
                            device_id_type=pl.DeviceIdType.MESH)

    for d in range(1, sections):
        greet(flipped(section, d), place)

    @pl.when(odd & has_above)
    def _():
        greet(section, place + 1)
        greet(section, place + 2)

    @pl.when(even)
    def _():
        greet(section, sibling)

    targets = sections - 1 + has_below.astype(jnp.int32) + lax.rem(place, 2)
    pl.semaphore_wait(barrier, targets)

    def slot(d):
        return d if group == 1 else flipped(section, d)

    def part(buffer, d):
        return buffer.at[pl.ds(slot(d) * local_tiles, local_tiles)]

    def remote(src, dst, send, recv, device):
        return pltpu.make_async_remote_copy(src_ref=src, dst_ref=dst, send_sem=send, recv_sem=recv,
                                            device_id=device, device_id_type=pl.DeviceIdType.MESH)

    def own_copy(d):
        to = flipped(section, d)
        at = d if group == 1 else section
        return remote(panels.at[:, to], own.at[pl.ds(at * local_tiles, local_tiles)], own_send.at[d],
                      own_recv.at[d], (to, place))

    def held(d):
        return panels.at[:, section] if d == 0 else part(own, d)

    def near_below(d):
        return remote(held(d), part(near, d), below_send.at[d], near_recv.at[d], (section, below))

    def far_below(d):
        return remote(held(d).at[:, pl.ds(0, far_count)], part(far, d), below_send.at[d], far_recv.at[d],
                      (section, below))

    def near_aside(d):
        return remote(held(d), part(near, d), near_send.at[d], near_recv.at[d], (section, sibling))

    def far_aside(d):
        return remote(part(near, d).at[:, pl.ds(0, far_count)], part(far, d), far_send.at[d], far_recv.at[d],
                      (section, sibling))

    def arrived(buffer, sems, d):
        pltpu.make_async_copy(part(buffer, d), part(buffer, d), sems.at[d]).wait()

    def onward(d):
        @pl.when(has_below & even)
        def _():
            near_below(d).start()

        @pl.when(has_below & odd)
        def _():
            far_below(d).start()

        @pl.when(odd)
        def _():
            near_aside(d).start()

    def transform(buffer, rowed, d):
        if group == 1:
            transform_tiles(buffer, fwd, lhs, rowed, d * segs, segs)
        elif d == sections - 1:
            transform_tiles(buffer, fwd, lhs, rowed, 0, SEGS)

    for d in range(1, sections):
        own_copy(d).start()
    keep = pltpu.make_async_copy(panels.at[:, section], part(own, 0), own_recv.at[0])
    keep.start()
    onward(0)
    table_copy.wait()
    keep.wait()
    for d in range(1, sections):
        transform(own, row_own, d - 1)
        arrived(own, own_recv, d)
        onward(d)
    transform(own, row_own, sections - 1)
    whiten_block(channels, row_own, white, 0)

    def take_near(d):
        arrived(near, near_recv, d)

        @pl.when(odd)
        def _():
            far_aside(d).start()

        transform(near, row_near, d)

    @pl.when(has_above)
    def _():
        for d in range(sections):
            take_near(d)
            arrived(far, far_recv, d)
            transform(far, row_far, d)
        whiten_block(channels, row_near, white, channels)
        whiten_block(far_count, row_far, white, 2 * channels)

    @pl.when((place >= places - 2) & even)
    def _():
        for d in range(sections):
            arrived(near, near_recv, d)
            transform(near, row_near, d)
        whiten_block(channels, row_near, white, channels)

    for d in range(sections):
        @pl.when(has_below & even)
        def _():
            near_below(d).wait_send()

        @pl.when(has_below & odd)
        def _():
            far_below(d).wait_send()

        @pl.when(odd)
        def _():
            near_aside(d).wait_send()

        @pl.when(odd & has_above)
        def _():
            far_aside(d).wait_send()

        if d > 0:
            own_copy(d).wait_send()


def gather(panels):
    local_tiles, sections, channels, _ = panels.shape
    tiles = local_tiles * sections
    far_count = -(-(NB - channels) // 16) * 16
    reach = 2 * channels + far_count
    dma = pltpu.SemaphoreType.DMA((sections,))
    return pl.pallas_call(
        gather_kernel,
        out_shape=jax.ShapeDtypeStruct((reach, ROWS, 128), jnp.bfloat16),
        in_specs=[pl.BlockSpec(memory_space=pltpu.HBM)] * 2,
        out_specs=pl.BlockSpec(memory_space=pltpu.VMEM),
        scratch_shapes=[
            pltpu.VMEM((SEG, 2 * SEG), jnp.bfloat16),
            pltpu.VMEM((tiles, channels, TILE), jnp.bfloat16),
            pltpu.VMEM((tiles, channels, TILE), jnp.bfloat16),
            pltpu.VMEM((tiles, far_count, TILE), jnp.bfloat16),
            pltpu.VMEM((SEGS * channels, SEG), jnp.bfloat16),
            pltpu.VMEM(((channels + 1) * ROW_PITCH, 128), jnp.float32),
            pltpu.VMEM(((channels + 1) * ROW_PITCH, 128), jnp.float32),
            pltpu.VMEM(((far_count + 1) * ROW_PITCH, 128), jnp.float32),
            pltpu.SemaphoreType.DMA, dma, dma, dma, dma, dma, dma, dma,
        ],
        compiler_params=pltpu.CompilerParams(
            vmem_limit_bytes=VMEM_BYTES, collective_id=0, has_side_effects=True),
        name="gather",
    )(panels, jnp.asarray(forward_table()))


def fold(tile):
    wide = tile.astype(jnp.float32)
    return wide[:8] + wide[8:]


def correlate_kernel(pairs_ref, count_ref, white, inv_hbm, out, inv, cross, stacks, table_sem, out_sems):
    owner = lax.axis_index("tm") * lax.axis_size("pairs") + lax.axis_index("pairs")
    offset = owner * CH_DEV
    table_copy = pltpu.make_async_copy(inv_hbm, inv, table_sem)
    table_copy.start()
    low_half = lax.broadcasted_iota(jnp.int32, (8, 128), 0) < 4
    half = ROWS // 2

    def one_pair(first, second):
        def left(part, t):
            return white[first, part * half + t * 16:part * half + (t + 1) * 16]

        def right(part, t):
            return white[second, part * half + t * 16:part * half + (t + 1) * 16]

        re, im = None, None
        for t in range(half // 16):
            lr, li, rr, ri = left(0, t), left(1, t), right(0, t), right(1, t)
            re_term = lr * rr + li * ri
            im_term = li * rr - lr * ri
            re = re_term if re is None else re + re_term
            im = im_term if im is None else im + im_term
        re, im = fold(re), fold(im)
        straight = jnp.where(low_half, re, im)
        crossed = jnp.where(low_half, im, re)
        return straight + pltpu.roll(crossed, 4, 0)

    def block_copy(block):
        rows = pl.ds(block * PAIR_BLOCK, PAIR_BLOCK)
        return pltpu.make_async_copy(stacks.at[rows], out.at[rows], out_sems.at[block])

    for block in range(out.shape[0] // PAIR_BLOCK):
        start = block * PAIR_BLOCK

        def some_pairs(step, carry):
            place = step * UNROLL
            ids = [(pairs_ref[0, start + place + u] - offset, pairs_ref[1, start + place + u] - offset)
                   for u in range(UNROLL)]
            results = [one_pair(first, second) for first, second in ids]
            for u in range(UNROLL):
                cross[pl.ds((place + u) * PAIR_PITCH, 8), :] = results[u]
            return carry

        lax.fori_loop(0, PAIR_BLOCK // UNROLL, some_pairs, 0)
        if block == 0:
            table_copy.wait()
        pieces = [cross[pl.ds(r, PAIR_BLOCK, stride=PAIR_PITCH), :].astype(jnp.bfloat16) for r in range(8)]
        lagged = jnp.dot(jnp.concatenate(pieces, axis=1), inv[...], preferred_element_type=jnp.float32)
        slots = start + lax.broadcasted_iota(jnp.int32, (PAIR_BLOCK, SEG), 0)
        stacks[start:start + PAIR_BLOCK, :] = jnp.where(slots < count_ref[0], lagged, 0.0)
        block_copy(block).start()

    for block in range(out.shape[0] // PAIR_BLOCK):
        block_copy(block).wait()


def correlate(pair_list, pair_count, white):
    capacity = pair_list.shape[1]
    smem = pl.BlockSpec(memory_space=pltpu.SMEM)
    vmem = pl.BlockSpec(memory_space=pltpu.VMEM)
    return pl.pallas_call(
        correlate_kernel,
        out_shape=jax.ShapeDtypeStruct((capacity, SEG), jnp.float32),
        in_specs=[smem, smem, vmem, pl.BlockSpec(memory_space=pltpu.HBM)],
        out_specs=pl.BlockSpec(memory_space=pl.ANY),
        scratch_shapes=[
            pltpu.VMEM((2 * SEG, SEG), jnp.bfloat16),
            pltpu.VMEM(((PAIR_BLOCK + 1) * PAIR_PITCH, 128), jnp.float32),
            pltpu.VMEM((capacity, SEG), jnp.float32),
            pltpu.SemaphoreType.DMA,
            pltpu.SemaphoreType.DMA((capacity // PAIR_BLOCK,)),
        ],
        compiler_params=pltpu.CompilerParams(vmem_limit_bytes=VMEM_BYTES),
        name="correlate",
    )(pair_list, pair_count, white, jnp.asarray(inverse_table()))


def per_device(panels, pair_list, pair_count):
    return correlate(pair_list, pair_count, gather(panels))


def solution(mesh):
    return jax.shard_map(
        per_device,
        mesh=mesh,
        in_specs=(P("tm", None, "pairs", None), P(None, ("tm", "pairs")), P(("tm", "pairs"))),
        out_specs=P(("tm", "pairs"), None),
        check_vma=False,
    )
```

```python
import math

import jax
import jax.numpy as jnp
import ml_dtypes
import numpy as np
from jax import lax
from jax.experimental import pallas as pl
from jax.experimental.pallas import tpu as pltpu
from jax.sharding import PartitionSpec as P

CH_DEV = 64
NB = 100
SEG = 512
SEGS = 12
TILE = 128
PER_SEG = SEG // TILE
KB = SEG // 128
ROWS = 2 * SEGS * KB
PAIR_BLOCK = 256
ROW_PITCH = ROWS + 1
PAIR_PITCH = 9
VMEM_BYTES = 40 * 1024 * 1024
UNROLL = 16


def forward_table():
    phase = np.outer(np.arange(SEG), np.arange(SEG)) % (2 * SEG) * (math.pi / SEG)
    table = np.concatenate([np.cos(phase), -np.sin(phase)], axis=1) / math.sqrt(SEG)
    return table.astype(np.float32).astype(ml_dtypes.bfloat16)


def inverse_table():
    phase = np.outer(np.arange(SEG), np.arange(SEG) - SEG // 2) % (2 * SEG) * (math.pi / SEG)
    weights = np.where(np.arange(SEG)[:, None] == 0, 1.0, 2.0) / math.sqrt(SEG) / SEGS
    table = np.concatenate([weights * np.cos(phase), -weights * np.sin(phase)], axis=0)
    return table.astype(np.float32).astype(ml_dtypes.bfloat16)


def transform_tiles(rows, fwd, lhs, rowed, first_seg, seg_count):
    count = rows.shape[1]
    for s in range(seg_count):
        tiles = [rows[(first_seg + s) * PER_SEG + q].astype(jnp.float32) for q in range(PER_SEG)]
        squares = sum(tile * tile for tile in tiles)
        gain = lax.rsqrt(jnp.sum(squares, axis=1, keepdims=True) / SEG + 1e-05)
        for q in range(PER_SEG):
            lhs[s * count:(s + 1) * count, q * TILE:(q + 1) * TILE] = (tiles[q] * gain).astype(jnp.bfloat16)
    for n in range(2 * SEG // 256):
        spectrum = jnp.dot(lhs[:seg_count * count], fwd[:, n * 256:(n + 1) * 256],
                           preferred_element_type=jnp.float32)
        for s in range(seg_count):
            for h in range(2):
                part, k = divmod(2 * n + h, KB)
                row = part * (ROWS // 2) + (first_seg + s) * KB + k
                rowed[pl.ds(row, count, stride=ROW_PITCH), :] = spectrum[s * count:(s + 1) * count,
                                                                         h * 128:(h + 1) * 128]


def whiten_block(count, rowed, white, base):
    def one_channel(c, carry):
        rows = rowed[pl.ds(c * ROW_PITCH, ROWS), :]
        tiles = [rows[t * 8:(t + 1) * 8] for t in range(ROWS // 8)]
        squares = [tile * tile for tile in tiles]
        while len(squares) > 1:
            odd_one = squares[len(squares) // 2 * 2:]
            squares = [squares[t] + squares[t + 1] for t in range(0, len(squares) - 1, 2)] + odd_one
        level = squares[0] + pltpu.roll(squares[0], 4, 0)
        gain = lax.rsqrt(level / SEGS + 0.5)
        white[base + c] = jnp.concatenate([tile * gain for tile in tiles], axis=0).astype(jnp.bfloat16)
        return carry

    lax.fori_loop(0, count, one_channel, 0, unroll=4)


def flipped(index, mask):
    bit = 1
    while bit <= mask:
        if mask & bit:
            index = index + bit * (1 - 2 * lax.rem(index // bit, 2))
        bit *= 2
    return index


def gather_kernel(panels, fwd_hbm, white, fwd, own, near, far, lhs, row_own, row_near, row_far,
                  table_sem, own_send, below_send, near_send, far_send, own_recv, near_recv, far_recv):
    section = lax.axis_index("tm")
    place = lax.axis_index("pairs")
    sections, places = lax.axis_size("tm"), lax.axis_size("pairs")
    local_tiles = panels.shape[0]
    channels, far_count = own.shape[1], far.shape[1]
    group = PER_SEG // math.gcd(PER_SEG, local_tiles)
    segs = local_tiles // PER_SEG
    odd = lax.rem(place, 2) == 1
    even = lax.rem(place, 2) == 0
    has_below = place >= 2
    has_above = place < places - 2
    below = place - 2 + lax.rem(place + 1, 2)
    sibling = place - 1 + 2 * lax.rem(place + 1, 2)

    table_copy = pltpu.make_async_copy(fwd_hbm, fwd, table_sem)
    table_copy.start()
    barrier = pltpu.get_barrier_semaphore()

    def greet(other_section, other_place):
        pl.semaphore_signal(barrier, inc=1, device_id=(other_section, other_place),
                            device_id_type=pl.DeviceIdType.MESH)

    for d in range(1, sections):
        greet(flipped(section, d), place)

    @pl.when(odd & has_above)
    def _():
        greet(section, place + 1)
        greet(section, place + 2)

    @pl.when(even)
    def _():
        greet(section, sibling)

    targets = sections - 1 + has_below.astype(jnp.int32) + lax.rem(place, 2)
    pl.semaphore_wait(barrier, targets)

    def slot(d):
        return d if group == 1 else flipped(section, d)

    def part(buffer, d):
        return buffer.at[pl.ds(slot(d) * local_tiles, local_tiles)]

    def remote(src, dst, send, recv, device):
        return pltpu.make_async_remote_copy(src_ref=src, dst_ref=dst, send_sem=send, recv_sem=recv,
                                            device_id=device, device_id_type=pl.DeviceIdType.MESH)

    def own_copy(d):
        to = flipped(section, d)
        at = d if group == 1 else section
        return remote(panels.at[:, to], own.at[pl.ds(at * local_tiles, local_tiles)], own_send.at[d],
                      own_recv.at[d], (to, place))

    def held(d):
        return panels.at[:, section] if d == 0 else part(own, d)

    def near_below(d):
        return remote(held(d), part(near, d), below_send.at[d], near_recv.at[d], (section, below))

    def far_below(d):
        return remote(held(d).at[:, pl.ds(0, far_count)], part(far, d), below_send.at[d], far_recv.at[d],
                      (section, below))

    def near_aside(d):
        return remote(held(d), part(near, d), near_send.at[d], near_recv.at[d], (section, sibling))

    def far_aside(d):
        return remote(part(near, d).at[:, pl.ds(0, far_count)], part(far, d), far_send.at[d], far_recv.at[d],
                      (section, sibling))

    def arrived(buffer, sems, d):
        pltpu.make_async_copy(part(buffer, d), part(buffer, d), sems.at[d]).wait()

    def onward(d):
        @pl.when(has_below & even)
        def _():
            near_below(d).start()

        @pl.when(has_below & odd)
        def _():
            far_below(d).start()

        @pl.when(odd)
        def _():
            near_aside(d).start()

    def transform(buffer, rowed, d):
        if group == 1:
            transform_tiles(buffer, fwd, lhs, rowed, d * segs, segs)
        elif d == sections - 1:
            transform_tiles(buffer, fwd, lhs, rowed, 0, SEGS)

    early = [d for d in range(1, sections) if d & (d - 1) == 0]
    late = [d for d in range(1, sections) if d & (d - 1) != 0]
    for d in early:
        own_copy(d).start()
    keep = pltpu.make_async_copy(panels.at[:, section], part(own, 0), own_recv.at[0])
    keep.start()
    onward(0)
    table_copy.wait()
    keep.wait()
    if group == 1:
        transform(own, row_own, 0)
    for d in early:
        arrived(own, own_recv, d)
        onward(d)
    for d in late:
        own_copy(d).start()
    if group == 1:
        for d in early:
            transform(own, row_own, d)
    for d in late:
        arrived(own, own_recv, d)
        onward(d)
        if group == 1:
            transform(own, row_own, d)
    if group > 1:
        transform(own, row_own, sections - 1)
    whiten_block(channels, row_own, white, 0)

    def take_near(d):
        arrived(near, near_recv, d)

        @pl.when(odd)
        def _():
            far_aside(d).start()

        transform(near, row_near, d)

    @pl.when(has_above)
    def _():
        for d in range(sections):
            take_near(d)
            arrived(far, far_recv, d)
            transform(far, row_far, d)
        whiten_block(channels, row_near, white, channels)
        whiten_block(far_count, row_far, white, 2 * channels)

    @pl.when((place >= places - 2) & even)
    def _():
        for d in range(sections):
            arrived(near, near_recv, d)
            transform(near, row_near, d)
        whiten_block(channels, row_near, white, channels)

    for d in range(sections):
        @pl.when(has_below & even)
        def _():
            near_below(d).wait_send()

        @pl.when(has_below & odd)
        def _():
            far_below(d).wait_send()

        @pl.when(odd)
        def _():
            near_aside(d).wait_send()

        @pl.when(odd & has_above)
        def _():
            far_aside(d).wait_send()

        if d > 0:
            own_copy(d).wait_send()


def gather(panels):
    local_tiles, sections, channels, _ = panels.shape
    tiles = local_tiles * sections
    far_count = -(-(NB - channels) // 16) * 16
    reach = 2 * channels + far_count
    dma = pltpu.SemaphoreType.DMA((sections,))
    return pl.pallas_call(
        gather_kernel,
        out_shape=jax.ShapeDtypeStruct((reach, ROWS, 128), jnp.bfloat16),
        in_specs=[pl.BlockSpec(memory_space=pltpu.HBM)] * 2,
        out_specs=pl.BlockSpec(memory_space=pltpu.VMEM),
        scratch_shapes=[
            pltpu.VMEM((SEG, 2 * SEG), jnp.bfloat16),
            pltpu.VMEM((tiles, channels, TILE), jnp.bfloat16),
            pltpu.VMEM((tiles, channels, TILE), jnp.bfloat16),
            pltpu.VMEM((tiles, far_count, TILE), jnp.bfloat16),
            pltpu.VMEM((SEGS * channels, SEG), jnp.bfloat16),
            pltpu.VMEM(((channels + 1) * ROW_PITCH, 128), jnp.float32),
            pltpu.VMEM(((channels + 1) * ROW_PITCH, 128), jnp.float32),
            pltpu.VMEM(((far_count + 1) * ROW_PITCH, 128), jnp.float32),
            pltpu.SemaphoreType.DMA, dma, dma, dma, dma, dma, dma, dma,
        ],
        compiler_params=pltpu.CompilerParams(
            vmem_limit_bytes=VMEM_BYTES, collective_id=0, has_side_effects=True),
        name="gather",
    )(panels, jnp.asarray(forward_table()))


def fold(tile):
    wide = tile.astype(jnp.float32)
    return wide[:8] + wide[8:]


def correlate_kernel(pairs_ref, count_ref, white, inv_hbm, out, inv, cross, stacks, table_sem, out_sems):
    owner = lax.axis_index("tm") * lax.axis_size("pairs") + lax.axis_index("pairs")
    offset = owner * CH_DEV
    table_copy = pltpu.make_async_copy(inv_hbm, inv, table_sem)
    table_copy.start()
    low_half = lax.broadcasted_iota(jnp.int32, (8, 128), 0) < 4
    half = ROWS // 2

    def one_pair(first, second):
        def left(part, t):
            return white[first, part * half + t * 16:part * half + (t + 1) * 16]

        def right(part, t):
            return white[second, part * half + t * 16:part * half + (t + 1) * 16]

        re, im = None, None
        for t in range(half // 16):
            lr, li, rr, ri = left(0, t), left(1, t), right(0, t), right(1, t)
            re_term = lr * rr + li * ri
            im_term = li * rr - lr * ri
            re = re_term if re is None else re + re_term
            im = im_term if im is None else im + im_term
        re, im = fold(re), fold(im)
        straight = jnp.where(low_half, re, im)
        crossed = jnp.where(low_half, im, re)
        return straight + pltpu.roll(crossed, 4, 0)

    def block_copy(block):
        rows = pl.ds(block * PAIR_BLOCK, PAIR_BLOCK)
        return pltpu.make_async_copy(stacks.at[rows], out.at[rows], out_sems.at[block])

    for block in range(out.shape[0] // PAIR_BLOCK):
        start = block * PAIR_BLOCK

        def some_pairs(step, carry):
            place = step * UNROLL
            ids = [(pairs_ref[0, start + place + u] - offset, pairs_ref[1, start + place + u] - offset)
                   for u in range(UNROLL)]
            results = [one_pair(first, second) for first, second in ids]
            for u in range(UNROLL):
                cross[pl.ds((place + u) * PAIR_PITCH, 8), :] = results[u]
            return carry

        lax.fori_loop(0, PAIR_BLOCK // UNROLL, some_pairs, 0)
        if block == 0:
            table_copy.wait()
        pieces = [cross[pl.ds(r, PAIR_BLOCK, stride=PAIR_PITCH), :].astype(jnp.bfloat16) for r in range(8)]
        lagged = jnp.dot(jnp.concatenate(pieces, axis=1), inv[...], preferred_element_type=jnp.float32)
        slots = start + lax.broadcasted_iota(jnp.int32, (PAIR_BLOCK, SEG), 0)
        stacks[start:start + PAIR_BLOCK, :] = jnp.where(slots < count_ref[0], lagged, 0.0)
        block_copy(block).start()

    for block in range(out.shape[0] // PAIR_BLOCK):
        block_copy(block).wait()


def correlate(pair_list, pair_count, white):
    capacity = pair_list.shape[1]
    smem = pl.BlockSpec(memory_space=pltpu.SMEM)
    vmem = pl.BlockSpec(memory_space=pltpu.VMEM)
    return pl.pallas_call(
        correlate_kernel,
        out_shape=jax.ShapeDtypeStruct((capacity, SEG), jnp.float32),
        in_specs=[smem, smem, vmem, pl.BlockSpec(memory_space=pltpu.HBM)],
        out_specs=pl.BlockSpec(memory_space=pl.ANY),
        scratch_shapes=[
            pltpu.VMEM((2 * SEG, SEG), jnp.bfloat16),
            pltpu.VMEM(((PAIR_BLOCK + 1) * PAIR_PITCH, 128), jnp.float32),
            pltpu.VMEM((capacity, SEG), jnp.float32),
            pltpu.SemaphoreType.DMA,
            pltpu.SemaphoreType.DMA((capacity // PAIR_BLOCK,)),
        ],
        compiler_params=pltpu.CompilerParams(vmem_limit_bytes=VMEM_BYTES),
        name="correlate",
    )(pair_list, pair_count, white, jnp.asarray(inverse_table()))


def per_device(panels, pair_list, pair_count):
    return correlate(pair_list, pair_count, gather(panels))


def solution(mesh):
    return jax.shard_map(
        per_device,
        mesh=mesh,
        in_specs=(P("tm", None, "pairs", None), P(None, ("tm", "pairs")), P(("tm", "pairs"))),
        out_specs=P(("tm", "pairs"), None),
        check_vma=False,
    )
```
